1024 devices in a mesh: gx: 32 (over z), gy: 8 (over y, x_lo), gz: 4 (over x_hi, core).
Axes of the slice: x: 4 (x_hi: 2, x_lo: 2; x = x_hi * 2 + x_lo), y: 4, z: 32, core: 2. Of those that a mesh axis runs over, the one named last changes fastest.
Arguments:
- load_parts: float32 [32, 8, 4, 602, 128], P('gx', 'gy', 'gz'), may hold values from -6 to 6
- schur_blocks: bfloat16 [32, 8, 4, 602, 602], P('gx', 'gy', 'gz'), may hold values from -0.13 to 3, as said below
- dirichlet_blocks: bfloat16 [32, 8, 4, 602, 602], P('gx', 'gy', 'gz'), may hold values from -0.06 to 1, as said below
- node_order: int32 [32, 8, 4, 602], P('gx', 'gy', 'gz'), may hold values from 0 to 1330, as said below
Outputs:
- solution: float32 [32, 8, 4, 602, 128], P('gx', 'gy', 'gz')
- residual: float32 [32, 8, 4, 602, 128], P('gx', 'gy', 'gz')
The draws below stay inside these ranges and needn't reach their ends.
Inputs may be any that keep to these rules, and one draw needn't show every extreme that they name: `node_order`: each subdomain's row lists every surface position of its 11 x 11 x 11 block exactly once, in an order of its own. `schur_blocks`: each subdomain's block is symmetric. `dirichlet_blocks`: each subdomain's block is symmetric.
All inputs are finite; a program needn't handle non-finite values.
Results may differ from the reference program's by a relative error of at most 0.007.
Values sent between devices are 32-bit elements; how exact they have to be, the bound alone decides.
A program may use at most 32 MiB of HBM per device.

```python
import math
import jax
import jax.numpy as jnp
from jax import lax

NODES = 11
IFACE = 602
NRHS = 128
ITERS = 2
SX = 32
SY = 8
SZ = 4


def surface_numbering(key):
    total = NODES ** 3
    flat_index = jnp.arange(total, dtype=jnp.int32)
    first = flat_index // (NODES * NODES)
    second = flat_index // NODES % NODES
    third = flat_index % NODES
    on_surface = (first == 0) | (first == NODES - 1) | (second == 0) | (second == NODES - 1) | (third == 0) | (third == NODES - 1)
    scores = jax.random.permutation(key, total).astype(jnp.int32)
    keyed = jnp.where(on_surface, scores, total + flat_index)
    return jnp.argsort(keyed, stable=True)[:IFACE].astype(jnp.int32)


def draw_node_order(key, part):
    key_list = jax.random.split(jax.random.fold_in(key, 11), SX * SY * SZ)
    return jax.vmap(surface_numbering)(key_list).reshape(SX, SY, SZ, IFACE)


def dense_block(key, lowest, highest, spread):
    noise_key, diag_key = jax.random.split(key)
    noise_draw = jnp.clip(jax.random.normal(noise_key, (IFACE, IFACE), jnp.float32), -6.0, 6.0)
    symmetric = (noise_draw + noise_draw.T) * (spread * 0.70710678)
    diagonal = jnp.exp(jax.random.uniform(diag_key, (IFACE,), jnp.float32, math.log(lowest), math.log(highest)))
    places = jnp.arange(IFACE)
    on_diagonal = places[:, None] == places[None, :]
    return jnp.where(on_diagonal, diagonal[None, :], symmetric)


def draw_schur_blocks(key, part):
    key_list = jax.random.split(jax.random.fold_in(key, 23), SX * SY * SZ)
    blocks = lax.map(lambda single: dense_block(single, 1.5, 3.0, 0.015), key_list)
    return blocks.reshape(SX, SY, SZ, IFACE, IFACE).astype(jnp.bfloat16)


def draw_dirichlet_blocks(key, part):
    key_list = jax.random.split(jax.random.fold_in(key, 37), SX * SY * SZ)
    blocks = lax.map(lambda single: dense_block(single, 0.5, 1.0, 0.006), key_list)
    return blocks.reshape(SX, SY, SZ, IFACE, IFACE).astype(jnp.bfloat16)


def level_of(own_key, shape, pieces, least, high):
    level, own = 1.0, jax.random.fold_in(own_key, 6)
    for dim, parts in pieces:
        heights = jnp.exp(jax.random.uniform(jax.random.fold_in(own, dim), (parts,), jnp.float32, least / len(pieces), high / len(pieces)))
        level = level * jnp.repeat(heights, shape[dim] // parts).reshape([-1 if axis == dim else 1 for axis in range(len(shape))])
    return level


def gaussian(key, dims, deviation, most, shards=(), held_as=jnp.bfloat16):
    array = deviation * jax.random.normal(key, dims, jnp.float32)
    if shards:
        array = array * level_of(key, dims, shards, -0.22, 0.18)
    return jnp.clip(array, -most, most).astype(held_as)


def setup_inputs(seed: int = 0) -> dict:
    key_of = jax.random.split(jax.random.key(seed), 5)
    return {
        "load_parts": gaussian(key_of[0], (SX, SY, SZ, IFACE, NRHS), 1.0, 6.0, ((0, 32), (1, 8), (2, 4)), jnp.float32),
        "schur_blocks": draw_schur_blocks(jax.random.fold_in(key_of[4], 71), 0),
        "dirichlet_blocks": draw_dirichlet_blocks(jax.random.fold_in(key_of[4], 71), 0),
        "node_order": draw_node_order(jax.random.fold_in(key_of[4], 71), 0),
    }


spectrum_low = 0.3
spectrum_high = 5.0


def node_counts(nsub):
    places = jnp.arange(NODES)[None, :]
    subs = jnp.arange(nsub)[:, None]
    lower = ((places == 0) & (subs > 0)).astype(jnp.float32)
    upper = ((places == NODES - 1) & (subs < nsub - 1)).astype(jnp.float32)
    return 1.0 + lower + upper


def surface_weights(orders_flat):
    count_x = node_counts(SX)
    count_y = node_counts(SY)
    count_z = node_counts(SZ)
    mult = count_x[:, None, None, :, None, None] * count_y[None, :, None, None, :, None] * count_z[None, None, :, None, None, :]
    mult = mult.reshape(SX * SY * SZ, NODES ** 3)
    picked = jnp.take_along_axis(mult, orders_flat, axis=1)
    return 1.0 / picked


def place_one(numbering, vector):
    return jnp.zeros((NODES ** 3, vector.shape[1]), vector.dtype).at[numbering].set(vector)


def pick_one(flat_cube, numbering):
    return flat_cube[numbering]


def join_axis(cubes, sub_axis, node_axis):
    first = lax.slice_in_dim(cubes, 0, 1, axis=node_axis)
    last = lax.slice_in_dim(cubes, NODES - 1, NODES, axis=node_axis)
    nsub = cubes.shape[sub_axis]
    zeros = jnp.zeros_like(lax.slice_in_dim(first, 0, 1, axis=sub_axis))
    from_lower = jnp.concatenate([zeros, lax.slice_in_dim(last, 0, nsub - 1, axis=sub_axis)], axis=sub_axis)
    from_upper = jnp.concatenate([lax.slice_in_dim(first, 1, nsub, axis=sub_axis), zeros], axis=sub_axis)
    shape = [1] * cubes.ndim
    shape[node_axis] = NODES
    places = jnp.arange(NODES)
    low_mark = (places == 0).astype(cubes.dtype).reshape(shape)
    high_mark = (places == NODES - 1).astype(cubes.dtype).reshape(shape)
    return cubes + low_mark * from_lower + high_mark * from_upper


def assemble(orders_flat, vectors):
    width = vectors.shape[2]
    cubes = jax.vmap(place_one)(orders_flat, vectors)
    cubes = cubes.reshape(SX, SY, SZ, NODES, NODES, NODES, width)
    cubes = join_axis(cubes, 0, 3)
    cubes = join_axis(cubes, 1, 4)
    cubes = join_axis(cubes, 2, 5)
    flat = cubes.reshape(SX * SY * SZ, NODES ** 3, width)
    return jax.vmap(pick_one)(flat, orders_flat)


def multiply(blocks, vectors):
    def single(pairing):
        return jnp.dot(pairing[0], pairing[1].astype(jnp.bfloat16), preferred_element_type=jnp.float32)
    return lax.map(single, (blocks, vectors))


def chebyshev(loads, schur_flat, dirichlet_flat, orders_flat, weight):
    theta = (spectrum_high + spectrum_low) / 2.0
    delta = (spectrum_high - spectrum_low) / 2.0
    sigma = theta / delta

    def precondition(vectors):
        return weight * assemble(orders_flat, multiply(dirichlet_flat, weight * vectors))

    solution = jnp.zeros_like(loads)
    residual = assemble(orders_flat, loads)
    rho_now = 1.0 / sigma
    direction = precondition(residual) / theta
    for index in range(ITERS):
        image = assemble(orders_flat, multiply(schur_flat, direction))
        solution = solution + direction
        residual = residual - image
        if index + 1 < ITERS:
            rho_next = 1.0 / (2.0 * sigma - rho_now)
            direction = rho_next * rho_now * direction + (2.0 * rho_next / delta) * precondition(residual)
            rho_now = rho_next
    return solution, residual


def reference(load_parts, schur_blocks, dirichlet_blocks, node_order):
    count = SX * SY * SZ
    orders_flat = node_order.reshape(count, IFACE).astype(jnp.int32)
    weight = surface_weights(orders_flat)[:, :, None]
    schur_flat = schur_blocks.reshape(count, IFACE, IFACE)
    dirichlet_flat = dirichlet_blocks.reshape(count, IFACE, IFACE)
    width = NRHS // 8
    blocks = load_parts.reshape(count, IFACE, 8, width).transpose(2, 0, 1, 3)

    def solve_block(loads):
        return chebyshev(loads, schur_flat, dirichlet_flat, orders_flat, weight)

    solution, residual = lax.map(solve_block, blocks)
    solution = solution.transpose(1, 2, 0, 3).reshape(SX, SY, SZ, IFACE, NRHS)
    residual = residual.transpose(1, 2, 0, 3).reshape(SX, SY, SZ, IFACE, NRHS)
    return (solution, residual)
```

```python
import functools
import itertools

import jax
import jax.numpy as jnp
import numpy as np
from jax import lax
from jax.experimental import pallas as pl
from jax.experimental.pallas import tpu as pltpu
from jax.sharding import PartitionSpec as P

NODES = 11
LAST = NODES - 1
AXES = ("gx", "gy", "gz")
MESH = pl.DeviceIdType.MESH

LOW = 0.3
HIGH = 5.0

FACES = [(0, -1, 0), (0, 1, 0), (0, 0, -1), (0, 0, 1), (-1, 0, 0), (1, 0, 0)]
EDGES = [d for d in itertools.product((-1, 0, 1), repeat=3) if sum(map(abs, d)) == 2]
CORNERS = [d for d in itertools.product((-1, 0, 1), repeat=3) if sum(map(abs, d)) == 3]
DIRS = FACES + EDGES + CORNERS
FACE_ROWS, EDGE_ROWS, CORNER_ROWS = 128, 16, 8
EDGE_AT = len(FACES) * FACE_ROWS
CORNER_AT = EDGE_AT + len(EDGES) * EDGE_ROWS
SENT = CORNER_AT + len(CORNERS) * CORNER_ROWS
RIM = 4 * LAST
INNER = FACE_ROWS - RIM
SKEL = 128
PRODUCED = SENT + SKEL
HELD = len(FACES) * INNER + SKEL
SKEL_AT = len(FACES) * INNER
SOURCES = len(FACES) * RIM + SENT - EDGE_AT


def start_of(k):
    if k < 6:
        return k * FACE_ROWS
    if k < 18:
        return EDGE_AT + (k - 6) * EDGE_ROWS
    return CORNER_AT + (k - 18) * CORNER_ROWS


def rows_of(k):
    return FACE_ROWS if k < 6 else EDGE_ROWS if k < 18 else CORNER_ROWS


def nodes_towards(direction):
    spans = [range(NODES) if c == 0 else ((0,) if c < 0 else (LAST,)) for c in direction]
    nodes = list(itertools.product(*spans))
    if sum(map(abs, direction)) == 1:
        free = [i for i in range(3) if direction[i] == 0]
        on_rim = lambda n: any(n[i] in (0, LAST) for i in free)
        nodes = [n for n in nodes if on_rim(n)] + [n for n in nodes if not on_rim(n)]
    return nodes


def tables():
    flat = lambda n: (n[0] * NODES + n[1]) * NODES + n[2]
    outer = lambda n: sum(c in (0, LAST) for c in n)
    skeleton = [n for n in itertools.product(range(NODES), repeat=3) if outer(n) >= 2]
    place = {n: s for s, n in enumerate(skeleton)}
    position = np.full(PRODUCED, -1, np.int32)
    source_of = np.full(SENT, -1, np.int64)
    for k, direction in enumerate(DIRS):
        for j, node in enumerate(nodes_towards(direction)):
            position[start_of(k) + j] = flat(node)
            if node in place:
                source_of[start_of(k) + j] = place[node]
    for s, node in enumerate(skeleton):
        position[SENT + s] = flat(node)
    rows = [start_of(k) + j for k in range(6) for j in range(RIM)] + list(range(EDGE_AT, SENT))
    gather = np.zeros((SKEL, SOURCES), np.float32)
    for column, row in enumerate(rows):
        if source_of[row] >= 0:
            gather[source_of[row], column] = 1.0
    side = np.zeros((3, SKEL), np.int32)
    for s, node in enumerate(skeleton):
        for axis in range(3):
            side[axis, s] = 1 if node[axis] == 0 else 2 if node[axis] == LAST else 0
    position = np.broadcast_to(position[:, None], (PRODUCED, 128))
    side = np.broadcast_to(side[:, :, None], (3, SKEL, 128))
    return position, gather, side


def split(value):
    high = value.astype(jnp.bfloat16)
    low = (value - high.astype(jnp.float32)).astype(jnp.bfloat16)
    return jnp.concatenate([high, low], axis=1)


def dot(a, b, dims=((1,), (0,))):
    return lax.dot_general(a, b, (dims, ((), ())), preferred_element_type=jnp.float32)


def kernel(
    sizes,
    loads_ref,
    schur_hbm,
    dirichlet_hbm,
    order_ref,
    position_ref,
    gather_ref,
    side_ref,
    solution_ref,
    residual_ref,
    schur_raw,
    dirichlet_raw,
    numbers,
    pick,
    half,
    schur,
    dirichlet,
    sent,
    got,
    weight,
    held_residual,
    held_direction,
    send_sem,
    recv_sem,
    load_sem,
):
    count = loads_ref.shape[0]
    get_schur = pltpu.make_async_copy(schur_hbm, schur_raw, load_sem.at[0])
    get_dirichlet = pltpu.make_async_copy(dirichlet_hbm, dirichlet_raw, load_sem.at[1])
    get_dirichlet.start()
    get_schur.start()

    place = [lax.axis_index(axis) for axis in AXES]
    has = {}
    for axis in range(3):
        has[axis, -1] = place[axis] > 0
        has[axis, 1] = place[axis] < sizes[axis] - 1

    def neighbour(direction):
        there, device = None, {}
        for axis in range(3):
            if direction[axis]:
                ok = has[axis, direction[axis]]
                there = ok if there is None else jnp.logical_and(there, ok)
                device[AXES[axis]] = jnp.clip(place[axis] + direction[axis], 0, sizes[axis] - 1)
        return there, device

    neighbours = [neighbour(direction) for direction in DIRS]
    opposite = [DIRS.index(tuple(-c for c in direction)) for direction in DIRS]

    got[...] = jnp.zeros_like(got)
    barrier = pltpu.get_barrier_semaphore()
    for there, device in neighbours:

        @pl.when(there)
        def _():
            pl.semaphore_signal(barrier, inc=1, device_id=device, device_id_type=MESH)

    def copy(k, slot):
        rows = pl.ds(start_of(k), rows_of(k))
        landing = pl.ds(start_of(opposite[k]), rows_of(k))
        return pltpu.make_async_remote_copy(
            src_ref=sent.at[slot, rows],
            dst_ref=got.at[slot, landing],
            send_sem=send_sem.at[slot, k],
            recv_sem=recv_sem.at[slot, opposite[k]],
            device_id=neighbours[k][1],
            device_id_type=MESH,
        )

    def send(slot):
        for k in range(len(DIRS)):

            @pl.when(neighbours[k][0])
            def _():
                copy(k, slot).start()

    def receive(slot):
        for k in range(len(DIRS)):

            @pl.when(neighbours[opposite[k]][0])
            def _():
                copy(k, slot).wait_recv()

    def finish(slot):
        for k in range(len(DIRS)):

            @pl.when(neighbours[k][0])
            def _():
                copy(k, slot).wait_send()

    def assembled(slot):
        parts = []
        for k in range(6):
            rows = pl.ds(start_of(k) + RIM, INNER)
            parts.append(sent[slot, rows, :] + got[slot, rows, :])
        rims = [got[slot, pl.ds(start_of(k), RIM), :] for k in range(6)]
        rims.append(got[slot, pl.ds(EDGE_AT, SENT - EDGE_AT), :])
        both = dot(gather_ref[...], split(jnp.concatenate(rims, axis=0)))
        own = sent[slot, pl.ds(SENT, SKEL), :]
        parts.append(own + (both[:, :128] + both[:, 128:]))
        return jnp.concatenate(parts, axis=0)

    def multiply(matrix, vector, slot):
        for block in range(PRODUCED // 384):
            rows = pl.ds(block * 384, 384)
            sent[slot, rows, :] = dot(matrix[rows, :], vector)

    def renumber(raw, matrix):
        for k in range(6):
            rows = pick[pl.ds(start_of(k) + RIM, INNER), pl.ds(0, count)]
            half[pl.ds(k * INNER, INNER), :] = dot(rows, raw[...]).astype(jnp.bfloat16)
        rows = pick[pl.ds(SENT, SKEL), pl.ds(0, count)]
        half[pl.ds(SKEL_AT, SKEL), :] = dot(rows, raw[...]).astype(jnp.bfloat16)

        def block(i, carry):
            rows = pl.ds(pl.multiple_of(i * 128, 128), 128)
            full = dot(pick[rows, pl.ds(0, count)], half[...], ((1,), (1,)))
            matrix[rows, :] = full.astype(jnp.bfloat16)
            return carry

        lax.fori_loop(0, PRODUCED // 128, block, 0)

    def place_back(value, out_ref):
        both = None
        pair = split(value)
        picks = [(start_of(k) + RIM, INNER, k * INNER) for k in range(6)] + [(SENT, SKEL, SKEL_AT)]
        rows = jnp.concatenate([pick[pl.ds(a, n), pl.ds(0, count)] for a, n, _ in picks], axis=0)
        both = dot(rows, pair, ((0,), (0,)))
        out_ref[...] = both[:, :128] + both[:, 128:]

    numbers[...] = jnp.full_like(numbers, -2)
    numbers[0:1, pl.ds(0, count)] = order_ref[...]
    for lane in range(numbers.shape[1] // 128):
        lanes = pl.ds(lane * 128, 128)
        same = position_ref[...] == numbers[0:1, lanes]
        pick[:, lanes] = same.astype(jnp.float32).astype(jnp.bfloat16)

    pair = split(loads_ref[...])
    for block in range(PRODUCED // 384):
        rows = pl.ds(block * 384, 384)
        both = dot(pick[rows, pl.ds(0, count)], pair)
        sent[0, rows, :] = both[:, :128] + both[:, 128:]

    around = 1
    for axis in range(3):
        around = around * (1 + has[axis, -1].astype(jnp.int32) + has[axis, 1].astype(jnp.int32))
    pl.semaphore_wait(barrier, around - 1)
    send(0)

    share = lambda ok: jnp.where(ok, 2.0, 1.0).astype(jnp.float32)
    for k in range(6):
        axis = [i for i in range(3) if FACES[k][i]][0]
        counted = jnp.full((INNER, 128), share(has[axis, FACES[k][axis]]), jnp.float32)
        weight[pl.ds(k * INNER, INNER), :] = 1.0 / counted
    counted = jnp.ones((SKEL, 128), jnp.float32)
    for axis in range(3):
        side = side_ref[axis]
        low, high = share(has[axis, -1]), share(has[axis, 1])
        counted = counted * jnp.where(side == 1, low, jnp.where(side == 2, high, 1.0))
    weight[pl.ds(SKEL_AT, SKEL), :] = 1.0 / counted

    theta = (HIGH + LOW) / 2.0
    delta = (HIGH - LOW) / 2.0
    sigma = theta / delta
    rho = 1.0 / sigma
    rho_next = 1.0 / (2.0 * sigma - rho)

    get_dirichlet.wait()
    renumber(dirichlet_raw, dirichlet)
    receive(0)
    held_residual[...] = assembled(0)

    multiply(dirichlet, (weight[...] * held_residual[...]).astype(jnp.bfloat16), 1)
    send(1)
    get_schur.wait()
    renumber(schur_raw, schur)
    finish(0)
    receive(1)
    held_direction[...] = weight[...] * assembled(1) / theta

    multiply(schur, held_direction[...].astype(jnp.bfloat16), 0)
    send(0)
    finish(1)
    receive(0)
    held_residual[...] = held_residual[...] - assembled(0)

    multiply(dirichlet, (weight[...] * held_residual[...]).astype(jnp.bfloat16), 1)
    send(1)
    finish(0)
    receive(1)
    former = held_direction[...]
    direction = rho_next * rho * former + (2.0 * rho_next / delta) * (weight[...] * assembled(1))
    held_direction[...] = former + direction

    multiply(schur, direction.astype(jnp.bfloat16), 0)
    send(0)
    place_back(held_direction[...], solution_ref)
    finish(1)
    receive(0)
    place_back(held_residual[...] - assembled(0), residual_ref)
    finish(0)


def on_device(sizes, load_parts, schur_blocks, dirichlet_blocks, node_order):
    count, columns = load_parts.shape[-2:]
    position, gather, side = tables()
    vmem = pl.BlockSpec(memory_space=pltpu.VMEM)
    hbm = pl.BlockSpec(memory_space=pl.ANY)
    padded = -(-count // 128) * 128
    bf16, f32 = jnp.bfloat16, jnp.float32
    out = jax.ShapeDtypeStruct((count, columns), f32)
    solution, residual = pl.pallas_call(
        functools.partial(kernel, sizes),
        out_shape=(out, out),
        in_specs=[vmem, hbm, hbm, vmem, vmem, vmem, vmem],
        out_specs=(vmem, vmem),
        scratch_shapes=[
            pltpu.VMEM((count, count), bf16),
            pltpu.VMEM((count, count), bf16),
            pltpu.VMEM((8, padded), jnp.int32),
            pltpu.VMEM((PRODUCED, padded), bf16),
            pltpu.VMEM((HELD, count), bf16),
            pltpu.VMEM((PRODUCED, HELD), bf16),
            pltpu.VMEM((PRODUCED, HELD), bf16),
            pltpu.VMEM((2, PRODUCED, columns), f32),
            pltpu.VMEM((2, SENT, columns), f32),
            pltpu.VMEM((HELD, columns), f32),
            pltpu.VMEM((HELD, columns), f32),
            pltpu.VMEM((HELD, columns), f32),
            pltpu.SemaphoreType.DMA((2, len(DIRS))),
            pltpu.SemaphoreType.DMA((2, len(DIRS))),
            pltpu.SemaphoreType.DMA((2,)),
        ],
        compiler_params=pltpu.CompilerParams(
            collective_id=0, has_side_effects=True, vmem_limit_bytes=40 << 20
        ),
        name="chebyshev",
    )(
        load_parts.reshape(count, columns),
        schur_blocks.reshape(count, count),
        dirichlet_blocks.reshape(count, count),
        node_order.reshape(1, count),
        jnp.asarray(position),
        jnp.asarray(gather, dtype=bf16),
        jnp.asarray(side),
    )
    return solution.reshape(load_parts.shape), residual.reshape(load_parts.shape)


def solution(mesh):
    sizes = tuple(mesh.shape[axis] for axis in AXES)
    in_specs = (
        P("gx", "gy", "gz", None, None),
        P("gx", "gy", "gz", None, None),
        P("gx", "gy", "gz", None, None),
        P("gx", "gy", "gz", None),
    )
    out_specs = (P("gx", "gy", "gz", None, None), P("gx", "gy", "gz", None, None))
    return jax.shard_map(
        functools.partial(on_device, sizes),
        mesh=mesh,
        in_specs=in_specs,
        out_specs=out_specs,
        check_vma=False,
    )
```

```python
import functools
import itertools

import jax
import jax.numpy as jnp
import numpy as np
from jax import lax
from jax.experimental import pallas as pl
from jax.experimental.pallas import tpu as pltpu
from jax.sharding import PartitionSpec as P

NODES = 11
LAST = NODES - 1
AXES = ("gx", "gy", "gz")
MESH = pl.DeviceIdType.MESH

LOW = 0.3
HIGH = 5.0

FACES = [(0, -1, 0), (0, 1, 0), (0, 0, -1), (0, 0, 1), (-1, 0, 0), (1, 0, 0)]
EDGES = [d for d in itertools.product((-1, 0, 1), repeat=3) if sum(map(abs, d)) == 2]
CORNERS = [d for d in itertools.product((-1, 0, 1), repeat=3) if sum(map(abs, d)) == 3]
DIRS = FACES + EDGES + CORNERS
EARLY = list(range(18, 26)) + list(range(6, 18)) + [0, 1]
LATE = [2, 3, 4, 5]
FACE_ROWS, EDGE_ROWS, CORNER_ROWS = 128, 16, 8
CORNER_AT = 0
EDGE_AT = CORNER_AT + len(CORNERS) * CORNER_ROWS
FACE_AT = EDGE_AT + len(EDGES) * EDGE_ROWS
SENT = FACE_AT + len(FACES) * FACE_ROWS
EARLY_ROWS = FACE_AT + 2 * FACE_ROWS
RIM = 4 * LAST
INNER = FACE_ROWS - RIM
SKEL = 128
PRODUCED = SENT + SKEL
HELD = len(FACES) * INNER + SKEL
SKEL_AT = len(FACES) * INNER
SOURCES = len(FACES) * RIM + FACE_AT


def start_of(k):
    if k < 6:
        return FACE_AT + k * FACE_ROWS
    if k < 18:
        return EDGE_AT + (k - 6) * EDGE_ROWS
    return CORNER_AT + (k - 18) * CORNER_ROWS


def rows_of(k):
    return NODES * NODES if k < 6 else NODES if k < 18 else 1


def nodes_towards(direction):
    spans = [range(NODES) if c == 0 else ((0,) if c < 0 else (LAST,)) for c in direction]
    nodes = list(itertools.product(*spans))
    if sum(map(abs, direction)) == 1:
        free = [i for i in range(3) if direction[i] == 0]
        on_rim = lambda n: any(n[i] in (0, LAST) for i in free)
        nodes = [n for n in nodes if on_rim(n)] + [n for n in nodes if not on_rim(n)]
    return nodes


def tables():
    flat = lambda n: (n[0] * NODES + n[1]) * NODES + n[2]
    outer = lambda n: sum(c in (0, LAST) for c in n)
    skeleton = [n for n in itertools.product(range(NODES), repeat=3) if outer(n) >= 2]
    place = {n: s for s, n in enumerate(skeleton)}
    position = np.full(PRODUCED, -1, np.int32)
    source_of = np.full(SENT, -1, np.int64)
    for k, direction in enumerate(DIRS):
        for j, node in enumerate(nodes_towards(direction)):
            position[start_of(k) + j] = flat(node)
            if node in place:
                source_of[start_of(k) + j] = place[node]
    for s, node in enumerate(skeleton):
        position[SENT + s] = flat(node)
    rows = [start_of(k) + j for k in range(6) for j in range(RIM)] + list(range(FACE_AT))
    gather = np.zeros((SKEL, SOURCES), np.float32)
    for column, row in enumerate(rows):
        if source_of[row] >= 0:
            gather[source_of[row], column] = 1.0
    side = np.zeros((3, SKEL), np.float32)
    for s, node in enumerate(skeleton):
        for axis in range(3):
            side[axis, s] = 1 if node[axis] == 0 else 2 if node[axis] == LAST else 0
    columns = np.zeros((16, 128), np.float32)
    columns[: PRODUCED // 128] = position.reshape(-1, 128)
    columns[PRODUCED // 128 : PRODUCED // 128 + 3] = side
    return columns, gather


def split(value):
    high = value.astype(jnp.bfloat16)
    low = (value - high.astype(jnp.float32)).astype(jnp.bfloat16)
    return jnp.concatenate([high, low], axis=1)


def dot(a, b, dims=((1,), (0,))):
    return lax.dot_general(a, b, (dims, ((), ())), preferred_element_type=jnp.float32)


def kernel(
    sizes,
    loads_hbm,
    schur_hbm,
    dirichlet_hbm,
    order_hbm,
    columns_hbm,
    gather_hbm,
    solution_ref,
    residual_ref,
    loads,
    schur_raw,
    dirichlet_raw,
    numbers,
    columns,
    gather,
    pick,
    half,
    schur,
    dirichlet,
    sent,
    got,
    weight,
    held_residual,
    held_direction,
    send_sem,
    recv_sem,
    load_sem,
):
    count = loads.shape[0]
    fetches = [
        pltpu.make_async_copy(source, target, load_sem.at[i])
        for i, (source, target) in enumerate(
            (
                (columns_hbm, columns),
                (order_hbm, numbers),
                (loads_hbm.at[:, 0, :], loads),
                (dirichlet_hbm, dirichlet_raw),
                (gather_hbm, gather),
                (schur_hbm, schur_raw),
            )
        )
    ]
    for fetch in fetches:
        fetch.start()

    place = [lax.axis_index(axis) for axis in AXES]
    has = {}
    for axis in range(3):
        has[axis, -1] = place[axis] > 0
        has[axis, 1] = place[axis] < sizes[axis] - 1

    def neighbour(direction):
        there, device = None, {}
        for axis in range(3):
            if direction[axis]:
                ok = has[axis, direction[axis]]
                there = ok if there is None else jnp.logical_and(there, ok)
                device[AXES[axis]] = jnp.clip(place[axis] + direction[axis], 0, sizes[axis] - 1)
        return there, device

    neighbours = [neighbour(direction) for direction in DIRS]
    opposite = [DIRS.index(tuple(-c for c in direction)) for direction in DIRS]

    got[...] = jnp.zeros_like(got)
    barrier = pltpu.get_barrier_semaphore()
    for there, device in neighbours:

        @pl.when(there)
        def _():
            pl.semaphore_signal(barrier, inc=1, device_id=device, device_id_type=MESH)

    def copy(k, slot):
        rows = pl.ds(start_of(k), rows_of(k))
        landing = pl.ds(start_of(opposite[k]), rows_of(k))
        return pltpu.make_async_remote_copy(
            src_ref=sent.at[slot, rows],
            dst_ref=got.at[slot, landing],
            send_sem=send_sem.at[slot, k],
            recv_sem=recv_sem.at[slot, opposite[k]],
            device_id=neighbours[k][1],
            device_id_type=MESH,
        )

    def send(slot, some):
        for k in some:

            @pl.when(neighbours[k][0])
            def _():
                copy(k, slot).start()

    def receive(slot):
        for k in range(len(DIRS)):

            @pl.when(neighbours[opposite[k]][0])
            def _():
                copy(k, slot).wait_recv()

    def finish(slot):
        for k in range(len(DIRS)):

            @pl.when(neighbours[k][0])
            def _():
                copy(k, slot).wait_send()

    def assembled(slot):
        parts = []
        for k in range(6):
            rows = pl.ds(start_of(k) + RIM, INNER)
            parts.append(sent[slot, rows, :] + got[slot, rows, :])
        rims = [got[slot, pl.ds(start_of(k), RIM), :] for k in range(6)]
        rims.append(got[slot, pl.ds(0, FACE_AT), :])
        both = dot(gather[...], split(jnp.concatenate(rims, axis=0)))
        own = sent[slot, pl.ds(SENT, SKEL), :]
        parts.append(own + (both[:, :128] + both[:, 128:]))
        return jnp.concatenate(parts, axis=0)

    def produce(rows_of_product, slot):
        for start, rows, some in ((0, EARLY_ROWS, EARLY), (EARLY_ROWS, SENT - EARLY_ROWS, LATE), (SENT, SKEL, [])):
            sent[slot, pl.ds(start, rows), :] = rows_of_product(pl.ds(start, rows))
            if slot == 0 and start == 0 and not started:
                started.append(True)
                pl.semaphore_wait(barrier, around - 1)
            send(slot, some)

    def multiply(matrix, vector, slot):
        produce(lambda rows: dot(matrix[rows, :], vector), slot)

    def renumber(raw, matrix):
        for k in range(6):
            rows = pick[pl.ds(start_of(k) + RIM, INNER), pl.ds(0, count)]
            half[pl.ds(k * INNER, INNER), :] = dot(rows, raw[...]).astype(jnp.bfloat16)
        rows = pick[pl.ds(SENT, SKEL), pl.ds(0, count)]
        half[pl.ds(SKEL_AT, SKEL), :] = dot(rows, raw[...]).astype(jnp.bfloat16)

        def block(i, carry):
            rows = pl.ds(pl.multiple_of(i * 128, 128), 128)
            full = dot(pick[rows, pl.ds(0, count)], half[...], ((1,), (1,)))
            matrix[rows, :] = full.astype(jnp.bfloat16)
            return carry

        lax.fori_loop(0, PRODUCED // 128, block, 0)

    def place_back(value, out_ref):
        both = None
        pair = split(value)
        picks = [(start_of(k) + RIM, INNER, k * INNER) for k in range(6)] + [(SENT, SKEL, SKEL_AT)]
        rows = jnp.concatenate([pick[pl.ds(a, n), pl.ds(0, count)] for a, n, _ in picks], axis=0)
        both = dot(rows, pair, ((0,), (0,)))
        out_ref[...] = both[:, :128] + both[:, 128:]

    around = 1
    for axis in range(3):
        around = around * (1 + has[axis, -1].astype(jnp.int32) + has[axis, 1].astype(jnp.int32))
    started = []

    fetches[0].wait()
    fetches[1].wait()
    upright = lambda row: jnp.broadcast_to(columns[pl.ds(row, 1), :], (128, 128)).T
    own = numbers[...].astype(jnp.float32)
    for block in range(PRODUCED // 128):
        position = upright(block)
        for at in range(0, count, 128):
            width = min(128, count - at)
            same = position[:, :width] == own[:, at : at + width]
            pick[pl.ds(block * 128, 128), pl.ds(at, width)] = same.astype(jnp.float32).astype(jnp.bfloat16)

    fetches[2].wait()
    pair = split(loads[...])

    def first_rows(rows):
        both = dot(pick[rows, pl.ds(0, count)], pair)
        return both[:, :128] + both[:, 128:]

    produce(first_rows, 0)

    share = lambda ok: jnp.where(ok, 2.0, 1.0).astype(jnp.float32)
    for k in range(6):
        axis = [i for i in range(3) if FACES[k][i]][0]
        counted = jnp.full((INNER, 128), share(has[axis, FACES[k][axis]]), jnp.float32)
        weight[pl.ds(k * INNER, INNER), :] = 1.0 / counted
    counted = jnp.ones((SKEL, 128), jnp.float32)
    for axis in range(3):
        side = upright(PRODUCED // 128 + axis)
        low, high = share(has[axis, -1]), share(has[axis, 1])
        counted = counted * jnp.where(side == 1, low, jnp.where(side == 2, high, 1.0))
    weight[pl.ds(SKEL_AT, SKEL), :] = 1.0 / counted

    theta = (HIGH + LOW) / 2.0
    delta = (HIGH - LOW) / 2.0
    sigma = theta / delta
    rho = 1.0 / sigma
    rho_next = 1.0 / (2.0 * sigma - rho)

    fetches[3].wait()
    fetches[4].wait()
    renumber(dirichlet_raw, dirichlet)
    receive(0)
    held_residual[...] = assembled(0)

    multiply(dirichlet, (weight[...] * held_residual[...]).astype(jnp.bfloat16), 1)
    fetches[5].wait()
    renumber(schur_raw, schur)
    finish(0)
    receive(1)
    held_direction[...] = weight[...] * assembled(1) / theta

    multiply(schur, held_direction[...].astype(jnp.bfloat16), 0)
    finish(1)
    receive(0)
    held_residual[...] = held_residual[...] - assembled(0)

    multiply(dirichlet, (weight[...] * held_residual[...]).astype(jnp.bfloat16), 1)
    finish(0)
    receive(1)
    former = held_direction[...]
    direction = rho_next * rho * former + (2.0 * rho_next / delta) * (weight[...] * assembled(1))
    held_direction[...] = former + direction

    multiply(schur, direction.astype(jnp.bfloat16), 0)
    place_back(held_direction[...], solution_ref)
    finish(1)
    receive(0)
    place_back(held_residual[...] - assembled(0), residual_ref)
    finish(0)


def hand_out(solution_in, residual_in, solution_out, residual_out, sem):
    copies = [
        pltpu.make_async_copy(solution_in, solution_out.at[:, 0, :], sem.at[0]),
        pltpu.make_async_copy(residual_in, residual_out.at[:, 0, :], sem.at[1]),
    ]
    for copy in copies:
        copy.start()
    for copy in copies:
        copy.wait()


def on_device(sizes, load_parts, schur_blocks, dirichlet_blocks, node_order):
    count, columns = load_parts.shape[-2:]
    table, gather = tables()
    vmem = pl.BlockSpec(memory_space=pltpu.VMEM)
    hbm = pl.BlockSpec(memory_space=pl.ANY)
    bf16, f32 = jnp.bfloat16, jnp.float32
    out = jax.ShapeDtypeStruct((count, columns), f32)
    solution, residual = pl.pallas_call(
        functools.partial(kernel, sizes),
        out_shape=(out, out),
        in_specs=[hbm] * 6,
        out_specs=(vmem, vmem),
        scratch_shapes=[
            pltpu.VMEM((count, columns), f32),
            pltpu.VMEM((count, count), bf16),
            pltpu.VMEM((count, count), bf16),
            pltpu.VMEM((1, count), jnp.int32),
            pltpu.VMEM((16, 128), f32),
            pltpu.VMEM((SKEL, SOURCES), bf16),
            pltpu.VMEM((PRODUCED, count), bf16),
            pltpu.VMEM((HELD, count), bf16),
            pltpu.VMEM((PRODUCED, HELD), bf16),
            pltpu.VMEM((PRODUCED, HELD), bf16),
            pltpu.VMEM((2, PRODUCED, columns), f32),
            pltpu.VMEM((2, SENT, columns), f32),
            pltpu.VMEM((HELD, columns), f32),
            pltpu.VMEM((HELD, columns), f32),
            pltpu.VMEM((HELD, columns), f32),
            pltpu.SemaphoreType.DMA((2, len(DIRS))),
            pltpu.SemaphoreType.DMA((2, len(DIRS))),
            pltpu.SemaphoreType.DMA((6,)),
        ],
        compiler_params=pltpu.CompilerParams(
            collective_id=0, has_side_effects=True, vmem_limit_bytes=60 << 20
        ),
        name="chebyshev",
    )(
        load_parts.reshape(count, 1, columns),
        schur_blocks.reshape(count, count),
        dirichlet_blocks.reshape(count, count),
        node_order.reshape(1, count),
        jnp.asarray(table),
        jnp.asarray(gather, dtype=bf16),
    )
    out = jax.ShapeDtypeStruct((count, 1, columns), f32)
    solution, residual = pl.pallas_call(
        hand_out,
        out_shape=(out, out),
        in_specs=[vmem, vmem],
        out_specs=(hbm, hbm),
        scratch_shapes=[pltpu.SemaphoreType.DMA((2,))],
        name="hand_out",
    )(solution, residual)
    return solution.reshape(load_parts.shape), residual.reshape(load_parts.shape)


def solution(mesh):
    sizes = tuple(mesh.shape[axis] for axis in AXES)
    in_specs = (
        P("gx", "gy", "gz", None, None),
        P("gx", "gy", "gz", None, None),
        P("gx", "gy", "gz", None, None),
        P("gx", "gy", "gz", None),
    )
    out_specs = (P("gx", "gy", "gz", None, None), P("gx", "gy", "gz", None, None))
    return jax.shard_map(
        functools.partial(on_device, sizes),
        mesh=mesh,
        in_specs=in_specs,
        out_specs=out_specs,
        check_vma=False,
    )
```

```python
import functools
import itertools

import jax
import jax.numpy as jnp
import numpy as np
from jax import lax
from jax.experimental import pallas as pl
from jax.experimental.pallas import tpu as pltpu
from jax.sharding import PartitionSpec as P

NODES = 11
LAST = NODES - 1
AXES = ("gx", "gy", "gz")
MESH = pl.DeviceIdType.MESH

LOW = 0.3
HIGH = 5.0

FACES = [(0, -1, 0), (0, 1, 0), (0, 0, -1), (0, 0, 1), (-1, 0, 0), (1, 0, 0)]
EDGES = [d for d in itertools.product((-1, 0, 1), repeat=3) if sum(map(abs, d)) == 2]
CORNERS = [d for d in itertools.product((-1, 0, 1), repeat=3) if sum(map(abs, d)) == 3]
DIRS = FACES + EDGES + CORNERS
SMALL = sorted(range(6, 26), key=lambda k: ((0, 1, -1).index(DIRS[k][2]) == 0, DIRS[k][2], -k))
EARLY = SMALL + [0, 1]
LATE = [2, 3, 4, 5]
ARRIVING = SMALL + [4, 5, 2, 3, 0, 1]
FACE_ROWS, EDGE_ROWS, CORNER_ROWS = 128, 16, 8
CORNER_AT = 0
EDGE_AT = CORNER_AT + len(CORNERS) * CORNER_ROWS
FACE_AT = EDGE_AT + len(EDGES) * EDGE_ROWS
SENT = FACE_AT + len(FACES) * FACE_ROWS
EARLY_ROWS = FACE_AT + 2 * FACE_ROWS
RIM = 4 * LAST
INNER = FACE_ROWS - RIM
SKEL = 128
PRODUCED = SENT + SKEL
HELD = len(FACES) * INNER + SKEL
SKEL_AT = len(FACES) * INNER
SOURCES = len(FACES) * RIM + FACE_AT


def start_of(k):
    if k < 6:
        return FACE_AT + k * FACE_ROWS
    if k < 18:
        return EDGE_AT + (k - 6) * EDGE_ROWS
    return CORNER_AT + (k - 18) * CORNER_ROWS


def rows_of(k):
    return NODES * NODES if k < 6 else NODES if k < 18 else 1


def nodes_towards(direction):
    spans = [range(NODES) if c == 0 else ((0,) if c < 0 else (LAST,)) for c in direction]
    nodes = list(itertools.product(*spans))
    if sum(map(abs, direction)) == 1:
        free = [i for i in range(3) if direction[i] == 0]
        on_rim = lambda n: any(n[i] in (0, LAST) for i in free)
        nodes = [n for n in nodes if on_rim(n)] + [n for n in nodes if not on_rim(n)]
    return nodes


def tables():
    flat = lambda n: (n[0] * NODES + n[1]) * NODES + n[2]
    outer = lambda n: sum(c in (0, LAST) for c in n)
    skeleton = [n for n in itertools.product(range(NODES), repeat=3) if outer(n) >= 2]
    place = {n: s for s, n in enumerate(skeleton)}
    position = np.full(PRODUCED, -1, np.int32)
    source_of = np.full(SENT, -1, np.int64)
    for k, direction in enumerate(DIRS):
        for j, node in enumerate(nodes_towards(direction)):
            position[start_of(k) + j] = flat(node)
            if node in place:
                source_of[start_of(k) + j] = place[node]
    for s, node in enumerate(skeleton):
        position[SENT + s] = flat(node)
    rows = [start_of(k) + j for k in range(6) for j in range(RIM)] + list(range(FACE_AT))
    gather = np.zeros((SKEL, SOURCES), np.float32)
    for column, row in enumerate(rows):
        if source_of[row] >= 0:
            gather[source_of[row], column] = 1.0
    side = np.zeros((3, SKEL), np.float32)
    for s, node in enumerate(skeleton):
        for axis in range(3):
            side[axis, s] = 1 if node[axis] == 0 else 2 if node[axis] == LAST else 0
    columns = np.zeros((16, 128), np.float32)
    columns[: PRODUCED // 128] = position.reshape(-1, 128)
    columns[PRODUCED // 128 : PRODUCED // 128 + 3] = side
    return columns, gather


def split(value):
    high = value.astype(jnp.bfloat16)
    low = (value - high.astype(jnp.float32)).astype(jnp.bfloat16)
    return jnp.concatenate([high, low], axis=1)


def dot(a, b, dims=((1,), (0,))):
    return lax.dot_general(a, b, (dims, ((), ())), preferred_element_type=jnp.float32)


def kernel(
    sizes,
    loads_hbm,
    schur_hbm,
    dirichlet_hbm,
    order_hbm,
    columns_hbm,
    gather_hbm,
    solution_ref,
    residual_ref,
    loads,
    schur_raw,
    dirichlet_raw,
    numbers,
    columns,
    gather,
    pick,
    held_pick,
    half,
    schur,
    dirichlet,
    sent,
    got,
    weight,
    held_residual,
    held_direction,
    send_sem,
    recv_sem,
    load_sem,
):
    count = loads.shape[0]
    fetches = [
        pltpu.make_async_copy(source, target, load_sem.at[i])
        for i, (source, target) in enumerate(
            (
                (columns_hbm, columns),
                (order_hbm, numbers),
                (loads_hbm.at[:, 0, :], loads),
                (dirichlet_hbm, dirichlet_raw),
                (gather_hbm, gather),
                (schur_hbm, schur_raw),
            )
        )
    ]
    for fetch in fetches:
        fetch.start()

    place = [lax.axis_index(axis) for axis in AXES]
    has = {}
    for axis in range(3):
        has[axis, -1] = place[axis] > 0
        has[axis, 1] = place[axis] < sizes[axis] - 1

    def neighbour(direction):
        there, device = None, {}
        for axis in range(3):
            if direction[axis]:
                ok = has[axis, direction[axis]]
                there = ok if there is None else jnp.logical_and(there, ok)
                device[AXES[axis]] = jnp.clip(place[axis] + direction[axis], 0, sizes[axis] - 1)
        return there, device

    neighbours = [neighbour(direction) for direction in DIRS]
    opposite = [DIRS.index(tuple(-c for c in direction)) for direction in DIRS]

    got[...] = jnp.zeros_like(got)
    barrier = pltpu.get_barrier_semaphore()
    for there, device in neighbours:

        @pl.when(there)
        def _():
            pl.semaphore_signal(barrier, inc=1, device_id=device, device_id_type=MESH)

    def copy(k, slot):
        rows = pl.ds(start_of(k), rows_of(k))
        landing = pl.ds(start_of(opposite[k]), rows_of(k))
        return pltpu.make_async_remote_copy(
            src_ref=sent.at[slot, rows],
            dst_ref=got.at[slot, landing],
            send_sem=send_sem.at[slot, k],
            recv_sem=recv_sem.at[slot, opposite[k]],
            device_id=neighbours[k][1],
            device_id_type=MESH,
        )

    inner = functools.reduce(jnp.logical_and, [has[axis, way] for axis in (0, 1) for way in (-1, 1)])

    def each(some, act):
        @pl.when(inner)
        def _():
            for way, run in itertools.groupby(some, lambda k: DIRS[k][2]):
                run = list(run)
                if way == 0:
                    for k in run:
                        act(k)
                else:

                    @pl.when(has[2, way])
                    def _():
                        for k in run:
                            act(k)

        @pl.when(jnp.logical_not(inner))
        def _():
            for k in some:
                pl.when(neighbours[k][0])(functools.partial(act, k))

    def send(slot, some):
        if some:
            each(some, lambda k: copy(k, slot).start())

    def receive(slot):
        each(ARRIVING, lambda k: copy(opposite[k], slot).wait_recv())

    def finish(slot):
        each(ARRIVING, lambda k: copy(k, slot).wait_send())

    def assembled(slot):
        parts = []
        for k in range(6):
            rows = pl.ds(start_of(k) + RIM, INNER)
            parts.append(sent[slot, rows, :] + got[slot, rows, :])
        rims = [got[slot, pl.ds(start_of(k), RIM), :] for k in range(6)]
        rims.append(got[slot, pl.ds(0, FACE_AT), :])
        both = dot(gather[...], split(jnp.concatenate(rims, axis=0)))
        own = sent[slot, pl.ds(SENT, SKEL), :]
        parts.append(own + (both[:, :128] + both[:, 128:]))
        return jnp.concatenate(parts, axis=0)

    def produce(rows_of_product, slot):
        for start, rows, some in ((0, EARLY_ROWS, EARLY), (EARLY_ROWS, SENT - EARLY_ROWS, LATE), (SENT, SKEL, [])):
            sent[slot, pl.ds(start, rows), :] = rows_of_product(pl.ds(start, rows))
            if slot == 0 and start == 0 and not started:
                started.append(True)
                pl.semaphore_wait(barrier, around - 1)
            send(slot, some)

    def multiply(matrix, vector, slot):
        produce(lambda rows: dot(matrix[rows, :], vector), slot)

    def renumber(raw, matrix):
        for at in range(0, count, 256):
            lanes = pl.ds(at, min(256, count - at))
            half[:, lanes] = dot(held_pick[...], raw[:, lanes]).astype(jnp.bfloat16)
        for at in range(0, HELD, 256):
            lanes = pl.ds(at, min(256, HELD - at))
            matrix[:, lanes] = dot(pick[...], half[lanes, :], ((1,), (1,))).astype(jnp.bfloat16)

    def place_back(value, out_ref):
        both = dot(held_pick[...], split(value), ((0,), (0,)))
        out_ref[...] = both[:, :128] + both[:, 128:]

    around = 1
    for axis in range(3):
        around = around * (1 + has[axis, -1].astype(jnp.int32) + has[axis, 1].astype(jnp.int32))
    started = []

    fetches[0].wait()
    fetches[1].wait()
    upright = lambda row: jnp.broadcast_to(columns[pl.ds(row, 1), :], (128, 128)).T
    own = numbers[...].astype(jnp.float32)
    pair = []

    def first_rows(rows):
        for block in range(rows.start // 128, (rows.start + rows.size) // 128):
            position = upright(block)
            for at in range(0, count, 128):
                width = min(128, count - at)
                same = position[:, :width] == own[:, at : at + width]
                pick[pl.ds(block * 128, 128), pl.ds(at, width)] = same.astype(jnp.float32).astype(jnp.bfloat16)
        if not pair:
            fetches[2].wait()
            pair.append(split(loads[...]))
        both = dot(pick[rows, pl.ds(0, count)], pair[0])
        return both[:, :128] + both[:, 128:]

    produce(first_rows, 0)
    for k in range(6):
        held_pick[pl.ds(k * INNER, INNER), :] = pick[pl.ds(start_of(k) + RIM, INNER), :]
    held_pick[pl.ds(SKEL_AT, SKEL), :] = pick[pl.ds(SENT, SKEL), :]

    share = lambda ok: jnp.where(ok, 2.0, 1.0).astype(jnp.float32)
    for k in range(6):
        axis = [i for i in range(3) if FACES[k][i]][0]
        counted = jnp.full((INNER, 128), share(has[axis, FACES[k][axis]]), jnp.float32)
        weight[pl.ds(k * INNER, INNER), :] = 1.0 / counted
    counted = jnp.ones((SKEL, 128), jnp.float32)
    for axis in range(3):
        side = upright(PRODUCED // 128 + axis)
        low, high = share(has[axis, -1]), share(has[axis, 1])
        counted = counted * jnp.where(side == 1, low, jnp.where(side == 2, high, 1.0))
    weight[pl.ds(SKEL_AT, SKEL), :] = 1.0 / counted

    theta = (HIGH + LOW) / 2.0
    delta = (HIGH - LOW) / 2.0
    sigma = theta / delta
    rho = 1.0 / sigma
    rho_next = 1.0 / (2.0 * sigma - rho)

    fetches[3].wait()
    fetches[4].wait()
    renumber(dirichlet_raw, dirichlet)
    receive(0)
    held_residual[...] = assembled(0)

    multiply(dirichlet, (weight[...] * held_residual[...]).astype(jnp.bfloat16), 1)
    fetches[5].wait()
    renumber(schur_raw, schur)
    finish(0)
    receive(1)
    held_direction[...] = weight[...] * assembled(1) / theta

    multiply(schur, held_direction[...].astype(jnp.bfloat16), 0)
    finish(1)
    receive(0)
    held_residual[...] = held_residual[...] - assembled(0)

    multiply(dirichlet, (weight[...] * held_residual[...]).astype(jnp.bfloat16), 1)
    finish(0)
    receive(1)
    former = held_direction[...]
    direction = rho_next * rho * former + (2.0 * rho_next / delta) * (weight[...] * assembled(1))
    held_direction[...] = former + direction

    multiply(schur, direction.astype(jnp.bfloat16), 0)
    place_back(held_direction[...], solution_ref)
    finish(1)
    receive(0)
    place_back(held_residual[...] - assembled(0), residual_ref)
    finish(0)


def hand_out(solution_in, residual_in, solution_out, residual_out, sem):
    copies = [
        pltpu.make_async_copy(solution_in, solution_out.at[:, 0, :], sem.at[0]),
        pltpu.make_async_copy(residual_in, residual_out.at[:, 0, :], sem.at[1]),
    ]
    for copy in copies:
        copy.start()
    for copy in copies:
        copy.wait()


def on_device(sizes, load_parts, schur_blocks, dirichlet_blocks, node_order):
    count, columns = load_parts.shape[-2:]
    table, gather = tables()
    vmem = pl.BlockSpec(memory_space=pltpu.VMEM)
    hbm = pl.BlockSpec(memory_space=pl.ANY)
    bf16, f32 = jnp.bfloat16, jnp.float32
    out = jax.ShapeDtypeStruct((count, columns), f32)
    solution, residual = pl.pallas_call(
        functools.partial(kernel, sizes),
        out_shape=(out, out),
        in_specs=[hbm] * 6,
        out_specs=(vmem, vmem),
        scratch_shapes=[
            pltpu.VMEM((count, columns), f32),
            pltpu.VMEM((count, count), bf16),
            pltpu.VMEM((count, count), bf16),
            pltpu.VMEM((1, count), jnp.int32),
            pltpu.VMEM((16, 128), f32),
            pltpu.VMEM((SKEL, SOURCES), bf16),
            pltpu.VMEM((PRODUCED, count), bf16),
            pltpu.VMEM((HELD, count), bf16),
            pltpu.VMEM((HELD, count), bf16),
            pltpu.VMEM((PRODUCED, HELD), bf16),
            pltpu.VMEM((PRODUCED, HELD), bf16),
            pltpu.VMEM((2, PRODUCED, columns), f32),
            pltpu.VMEM((2, SENT, columns), f32),
            pltpu.VMEM((HELD, columns), f32),
            pltpu.VMEM((HELD, columns), f32),
            pltpu.VMEM((HELD, columns), f32),
            pltpu.SemaphoreType.DMA((2, len(DIRS))),
            pltpu.SemaphoreType.DMA((2, len(DIRS))),
            pltpu.SemaphoreType.DMA((6,)),
        ],
        compiler_params=pltpu.CompilerParams(
            collective_id=0, has_side_effects=True, vmem_limit_bytes=60 << 20
        ),
        name="chebyshev",
    )(
        load_parts.reshape(count, 1, columns),
        schur_blocks.reshape(count, count),
        dirichlet_blocks.reshape(count, count),
        node_order.reshape(1, count),
        jnp.asarray(table),
        jnp.asarray(gather, dtype=bf16),
    )
    out = jax.ShapeDtypeStruct((count, 1, columns), f32)
    solution, residual = pl.pallas_call(
        hand_out,
        out_shape=(out, out),
        in_specs=[vmem, vmem],
        out_specs=(hbm, hbm),
        scratch_shapes=[pltpu.SemaphoreType.DMA((2,))],
        name="hand_out",
    )(solution, residual)
    return solution.reshape(load_parts.shape), residual.reshape(load_parts.shape)


def solution(mesh):
    sizes = tuple(mesh.shape[axis] for axis in AXES)
    in_specs = (
        P("gx", "gy", "gz", None, None),
        P("gx", "gy", "gz", None, None),
        P("gx", "gy", "gz", None, None),
        P("gx", "gy", "gz", None),
    )
    out_specs = (P("gx", "gy", "gz", None, None), P("gx", "gy", "gz", None, None))
    return jax.shard_map(
        functools.partial(on_device, sizes),
        mesh=mesh,
        in_specs=in_specs,
        out_specs=out_specs,
        check_vma=False,
    )
```
